32 devices in a mesh: fsdp: 8 (over z, y), slide: 4 (over x, core).
Axes of the slice: x: 2, y: 2, z: 4, core: 2. Of those that a mesh axis runs over, the one named last changes fastest.
Arguments:
- tiles: bfloat16 [16384, 1536], P(('slide', 'fsdp')), parts along dimension 0, may hold values from -6 to 6
- tile_cell: int32 [16384], P('slide'), parts along dimension 0, may hold values from 0 to 4095, as said below
- tissue: int32 [64, 256], P('slide'), parts along dimension 0, may hold values 0 or 1
- norm_gain: float32 [2, 1536], replicated, may hold values from 0.5 to 1.5
- qk_gain: float32 [2, 2, 64], replicated, may hold values from 0.5 to 4
- row_qkv: bfloat16 [1536, 4608], P(None, 'fsdp'), may hold values from -0.15625 to 0.15625
- row_out: bfloat16 [1536, 1536], P(None, 'fsdp'), may hold values from -0.15625 to 0.15625
- col_qkv: bfloat16 [1536, 4608], P(None, 'fsdp'), may hold values from -0.15625 to 0.15625
- col_out: bfloat16 [1536, 1536], P(None, 'fsdp'), may hold values from -0.15625 to 0.15625
Outputs:
- encoded: bfloat16 [64, 256, 1536], P('slide', 'fsdp'), parts along dimension 0
The draws below stay inside these ranges and needn't reach their ends.
There are 4 independent parts, one for each index of `slide`. The reference program is written for one: setup_inputs(seed, part) draws one part's arguments, and reference() takes and returns one part's arrays. A program takes and returns all parts, laid end to end along the dimension named above; an argument that names none is the same for every part. Nothing has to cross between parts.
Inputs may be any that keep to these rules, and one draw needn't show every extreme that they name: Slots d * 512 + b * 64 up to d * 512 + (b + 1) * 64 - 1 hold tiles of grid rows b * 2 to (b + 1) * 2 - 1; tile_cell names every grid cell exactly once.
All inputs are finite; a program needn't handle non-finite values.
Results may differ from the reference program's by a relative error of at most 0.02.
The reference program's roundings to bfloat16 on the way count: a program that leaves them out, or rounds other values in their place, can miss the bound.
Values may be sent and summed in bfloat16 or wider, within the bound.
A program may use at most 256 MiB of HBM per device.

```python
import jax
import jax.numpy as jnp
from jax import lax

D = 1536
HEADS = 24
HS = 64
COLS = 256
ROWS_DEV = 2
GRID_R = 16
TOKENS = 4096
N_FSDP = 8


def draw_tile_cell(key, part):
    count = N_FSDP
    tok_dev = ROWS_DEV * COLS
    slots = tok_dev // count
    scores = jax.random.randint(jax.random.fold_in(key, 7), (count, tok_dev), 0, 65536) * tok_dev
    scores = scores + jnp.arange(tok_dev, dtype=jnp.int32)[None, :]
    local = jnp.argsort(scores, axis=1, stable=True).astype(jnp.int32)
    cells = jnp.arange(count, dtype=jnp.int32)[:, None] * tok_dev + local
    cells = cells.reshape(count, count, slots).transpose(1, 0, 2).reshape(-1)
    return cells.astype(jnp.int32)


def draw_qk_gain(key, part):
    values = jax.random.uniform(jax.random.fold_in(key, 11), (2, 2, HS), jnp.float32, 0.6, 1.4)
    return values.astype(jnp.float32)


def touch_ends(array, rng, low, largest):
    extent = array.shape
    index_at = [jax.random.randint(jax.random.fold_in(rng, axis), (), 0, extent[axis]) for axis in range(len(extent))]
    array = array.at[tuple(index_at)].set(low)
    longest = extent.index(max(extent))
    index_at[longest] = (index_at[longest] + 1) % extent[longest]
    return array.at[tuple(index_at)].set(largest)


def block_scale(stream_key, dims, shards, low, top_value):
    factor_of, own = 1.0, jax.random.fold_in(stream_key, 6)
    for dim, shards_of in shards:
        steps = jnp.exp(jax.random.uniform(jax.random.fold_in(own, dim), (shards_of,), jnp.float32, low / len(shards), top_value / len(shards)))
        factor_of = factor_of * jnp.repeat(steps, dims[dim] // shards_of).reshape([-1 if axis == dim else 1 for axis in range(len(dims))])
    return factor_of


def noise(rng, shape, spread, most, pieces=(), kind=jnp.bfloat16):
    values = spread * jax.random.normal(rng, shape, jnp.float32)
    if pieces:
        values = values * block_scale(rng, shape, pieces, -0.22, 0.18)
    return jnp.clip(values, -most, most).astype(kind)


def setup_inputs(seed: int = 0, part: int = 0) -> dict:
    splits = jax.random.split(jax.random.key(seed), 10)
    part_keys = jax.random.split(jax.random.fold_in(splits[9], part), 10)
    return {
        "tiles": noise(part_keys[0], (TOKENS, D), 1.0, 6.0, ((0, 8),)),
        "tile_cell": draw_tile_cell(jax.random.fold_in(jax.random.fold_in(splits[9], part), 71), part),
        "tissue": touch_ends((jax.random.randint(part_keys[2], (GRID_R, COLS), 0, 5) < 3).astype(jnp.int32), jax.random.fold_in(part_keys[2], 1), 0, 1),
        "norm_gain": jnp.clip(1.0 + 0.1 * jax.random.normal(splits[3], (2, D), jnp.float32), 0.5, 1.5),
        "qk_gain": draw_qk_gain(jax.random.fold_in(splits[9], 71), part),
        "row_qkv": noise(splits[5], (D, 3 * D), D ** -0.5, 0.15625, ((1, 8),)),
        "row_out": noise(splits[6], (D, D), D ** -0.5, 0.15625, ((1, 8),)),
        "col_qkv": noise(splits[7], (D, 3 * D), D ** -0.5, 0.15625, ((1, 8),)),
        "col_out": noise(splits[8], (D, D), D ** -0.5, 0.15625, ((1, 8),)),
    }


EPS = 1e-06

def rms_norm(grid, gain):
    values = grid.astype(jnp.float32)
    scale = lax.rsqrt(lax.optimization_barrier(jnp.mean(values * values, axis=-1, keepdims=True)) + EPS)
    return (values * scale * gain).astype(jnp.bfloat16)

def head_norm(values, gain):
    scale = lax.rsqrt(lax.optimization_barrier(jnp.mean(values * values, axis=-1, keepdims=True)) + EPS)
    return values * scale * gain

def rotate(values, rows_pos, cols_pos):
    quarter = values.shape[-1] // 4
    freq = 10000.0 ** (-jnp.arange(quarter).astype(jnp.float32) / quarter)

    def turn(part, position):
        angle = position.astype(jnp.float32)[..., None, None] * freq
        cosine = jnp.cos(angle)
        sine = jnp.sin(angle)
        first = part[..., :quarter]
        second = part[..., quarter:]
        return jnp.concatenate([first * cosine - second * sine, first * sine + second * cosine], axis=-1)
    half = 2 * quarter
    return jnp.concatenate([turn(values[..., :half], rows_pos), turn(values[..., half:], cols_pos)], axis=-1)

def attend(qkv, gains, rows_pos, cols_pos, keys_live, column, heads):
    width = qkv.shape[-1] // 3
    size = width // heads
    shape = qkv.shape[:-1] + (heads, size)
    query = qkv[..., :width].reshape(shape).astype(jnp.float32)
    key = qkv[..., width:2 * width].reshape(shape).astype(jnp.float32)
    value = qkv[..., 2 * width:].reshape(shape).astype(jnp.float32)
    query = lax.optimization_barrier(rotate(head_norm(query, gains[0]), rows_pos, cols_pos).astype(jnp.bfloat16))
    key = lax.optimization_barrier(rotate(head_norm(key, gains[1]), rows_pos, cols_pos).astype(jnp.bfloat16))
    if column:
        score_form = 'lbhd,mbhd->bhlm'
        mix_form = 'bhlm,mbhd->lbhd'
        live = keys_live.T
    else:
        score_form = 'blhd,bmhd->bhlm'
        mix_form = 'bhlm,bmhd->blhd'
        live = keys_live
    scores = jnp.einsum(score_form, query.astype(jnp.float32), key.astype(jnp.float32)) * size ** (-0.5)
    length = scores.shape[-1]
    diagonal = jnp.arange(length)[:, None] == jnp.arange(length)[None, :]
    allow = (live[:, None, None, :] > 0) | diagonal[None, None]
    scores = jnp.where(allow, scores, -1e+30)
    top = lax.optimization_barrier(jnp.max(scores, axis=-1, keepdims=True))
    weights = jnp.exp(scores - top)
    total = lax.optimization_barrier(jnp.sum(weights, axis=-1))
    rounded = lax.optimization_barrier(weights.astype(jnp.bfloat16))
    mixed = jnp.einsum(mix_form, rounded.astype(jnp.float32), value)
    if column:
        total = total.transpose(2, 0, 1)
    else:
        total = total.transpose(0, 2, 1)
    return (mixed / total[..., None]).reshape(qkv.shape[:-1] + (width,)).astype(jnp.bfloat16)

def reference(tiles, tile_cell, tissue, norm_gain, qk_gain, row_qkv, row_out, col_qkv, col_out):
    cells = tile_cell.astype(jnp.int32)
    grid = jnp.zeros((TOKENS, D), jnp.bfloat16).at[cells].set(tiles)
    rows_pos = lax.broadcasted_iota(jnp.int32, (GRID_R, COLS), 0)
    cols_pos = lax.broadcasted_iota(jnp.int32, (GRID_R, COLS), 1)
    qkv = jnp.dot(rms_norm(grid, norm_gain[0]), row_qkv, preferred_element_type=jnp.float32)
    qkv = qkv.astype(jnp.bfloat16).reshape(GRID_R, COLS, 3 * D)

    def one_row(items):
        line, row_p, col_p, live = items
        return attend(line[None], qk_gain[0], row_p[None], col_p[None], live[None], False, HEADS)[0]
    mixed = lax.map(one_row, (qkv, rows_pos, cols_pos, tissue))
    hidden = grid.astype(jnp.float32) + jnp.dot(mixed.reshape(TOKENS, D), row_out, preferred_element_type=jnp.float32)
    hidden = hidden.astype(jnp.bfloat16)
    qkv_col = jnp.dot(rms_norm(hidden, norm_gain[1]), col_qkv, preferred_element_type=jnp.float32)
    qkv_col = qkv_col.astype(jnp.bfloat16).reshape(GRID_R, COLS, 3 * D)
    mixed_col = attend(qkv_col, qk_gain[1], rows_pos, cols_pos, tissue, True, HEADS)
    result = hidden.astype(jnp.float32) + jnp.dot(mixed_col.reshape(TOKENS, D), col_out, preferred_element_type=jnp.float32)
    return result.astype(jnp.bfloat16).reshape(GRID_R, COLS, D)
```

```python
import functools

import jax
import jax.numpy as jnp
from jax import lax
from jax.experimental import pallas as pl
from jax.experimental.pallas import tpu as pltpu
from jax.sharding import PartitionSpec as P

HEADS = 24
MESH = pl.DeviceIdType.MESH


EPS = 1e-06


def rms_norm(grid, gain):
    values = grid.astype(jnp.float32)
    scale = lax.rsqrt(jnp.mean(values * values, axis=-1, keepdims=True) + EPS)
    return (values * scale * gain).astype(jnp.bfloat16)


def head_norm(values, gain):
    scale = lax.rsqrt(jnp.mean(values * values, axis=-1, keepdims=True) + EPS)
    return values * scale * gain


def rotate(values, rows_pos, cols_pos):
    quarter = values.shape[-1] // 4
    freq = 10000.0 ** (-jnp.arange(quarter).astype(jnp.float32) / quarter)

    def turn(part, position):
        angle = position.astype(jnp.float32)[..., None, None] * freq
        cosine = jnp.cos(angle)
        sine = jnp.sin(angle)
        first = part[..., :quarter]
        second = part[..., quarter:]
        return jnp.concatenate(
            [first * cosine - second * sine, first * sine + second * cosine], axis=-1
        )

    half = 2 * quarter
    return jnp.concatenate(
        [turn(values[..., :half], rows_pos), turn(values[..., half:], cols_pos)], axis=-1
    )


def attend(qkv, gains, rows_pos, cols_pos, keys_live, column, heads):
    width = qkv.shape[-1] // 3
    size = width // heads
    shape = qkv.shape[:-1] + (heads, size)
    query = qkv[..., :width].reshape(shape).astype(jnp.float32)
    key = qkv[..., width : 2 * width].reshape(shape).astype(jnp.float32)
    value = qkv[..., 2 * width :].reshape(shape)
    query = rotate(head_norm(query, gains[0]), rows_pos, cols_pos).astype(jnp.bfloat16)
    key = rotate(head_norm(key, gains[1]), rows_pos, cols_pos).astype(jnp.bfloat16)
    if column:
        score_form = "lbhd,mbhd->bhlm"
        mix_form = "bhlm,mbhd->lbhd"
        live = keys_live.T
    else:
        score_form = "blhd,bmhd->bhlm"
        mix_form = "bhlm,bmhd->blhd"
        live = keys_live
    scores = jnp.einsum(score_form, query, key, preferred_element_type=jnp.float32) * size ** (-0.5)
    length = scores.shape[-1]
    diagonal = jnp.arange(length)[:, None] == jnp.arange(length)[None, :]
    allow = (live[:, None, None, :] > 0) | diagonal[None, None]
    scores = jnp.where(allow, scores, -1e30)
    top = jnp.max(scores, axis=-1, keepdims=True)
    weights = jnp.exp(scores - top)
    total = jnp.sum(weights, axis=-1)
    mixed = jnp.einsum(
        mix_form, weights.astype(jnp.bfloat16), value, preferred_element_type=jnp.float32
    )
    if column:
        total = total.transpose(2, 0, 1)
    else:
        total = total.transpose(0, 2, 1)
    return (mixed / total[..., None]).reshape(qkv.shape[:-1] + (width,)).astype(jnp.bfloat16)


def project_qkv(normed, weight):
    if weight.ndim == 3:
        return stacked(normed, weight).astype(jnp.bfloat16)

    def multiply(piece, start):
        return jnp.dot(normed, piece, preferred_element_type=jnp.float32)

    return multiply(lax.all_gather(weight, "fsdp", axis=1, tiled=True), jnp.int32(0)).astype(
        jnp.bfloat16
    )


def project_out(mixed, weight):
    if weight.ndim == 3:
        return stacked(mixed, weight)

    def multiply(piece, start):
        return jnp.dot(mixed, piece, preferred_element_type=jnp.float32)

    return multiply(lax.all_gather(weight, "fsdp", axis=1, tiled=True), jnp.int32(0))


def gather_kernel(n, part, *refs):
    ws, outs = refs[:n], refs[n:2*n]
    loc, send, zr, yr, xr, cr = refs[2*n:]
    s, f = lax.axis_index("slide"), lax.axis_index("fsdp")
    x, c, z, y = s // 2, s % 2, f // 2, f % 2
    zdev = lambda d: (lax.rem(z + d, 4) * 2 + y, s)
    ydev = (z * 2 + 1 - y, s)
    xdev = (f, (1 - x) * 2 + c)
    cdev = (f, x * 2 + 1 - c)
    bar = pltpu.get_barrier_semaphore()
    peers = [zdev(1), zdev(2), zdev(3), ydev, xdev, cdev]
    for p in peers:
        pl.semaphore_signal(bar, inc=1, device_id=p, device_id_type=MESH)
    pl.semaphore_wait(bar, len(peers))
    sends = []
    rows = ws[0].shape[0]
    rest = (rows - 4 * part) // 2
    def span(k, ax, ac):
        if k == 0:
            return pl.ds(pl.multiple_of((ax * 2 + ac) * part, 16), part)
        return pl.ds(pl.multiple_of(4 * part + ac * rest, 16), rest)
    kinds = (0, 1) if rest else (0,)
    count = [0] * n
    def push(a, src, fsrc, sp, dev, rsem):
        cp = pltpu.make_async_remote_copy(src_ref=src, dst_ref=outs[a].at[fsrc, sp], send_sem=send.at[a, count[a]],
            recv_sem=rsem, device_id=dev, device_id_type=MESH)
        count[a] += 1
        cp.start()
        sends.append(cp)
    def arrived(a, fsrc, sp, rsem):
        r = outs[a].at[fsrc, sp]
        pltpu.make_async_remote_copy(src_ref=r, dst_ref=r, send_sem=send.at[a, 0], recv_sem=rsem, device_id=cdev, device_id_type=MESH).wait_recv()
    local = []
    for a in range(n):
        for k in kinds:
            sp = span(k, x, c)
            for d in (1, 3, 2):
                push(a, ws[a].at[sp], f, sp, zdev(d), zr.at[a, k, d - 1])
            push(a, ws[a].at[sp], f, sp, ydev, yr.at[a, k, 0])
        cp = pltpu.make_async_copy(ws[a], outs[a].at[f], loc.at[a])
        cp.start()
        local.append(cp)
    zf = lambda d: lax.rem(z - d + 4, 4) * 2 + y
    yf = lambda d: lax.rem(z - d + 4, 4) * 2 + 1 - y
    def stage_z(a):
        for d in (1, 3, 2):
            fs = zf(d)
            for k in kinds:
                sp = span(k, x, c)
                arrived(a, fs, sp, zr.at[a, k, d - 1])
                o = outs[a].at[fs, sp]
                push(a, o, fs, sp, ydev, yr.at[a, k, d])
                if k == 0:
                    push(a, o, fs, sp, xdev, xr.at[a, d - 1])
                push(a, o, fs, sp, cdev, cr.at[a, k, d - 1])
    def stage_y(a):
        for d in (0, 1, 3, 2):
            fs = yf(d)
            for k in kinds:
                sp = span(k, x, c)
                arrived(a, fs, sp, yr.at[a, k, d])
                o = outs[a].at[fs, sp]
                if k == 0:
                    push(a, o, fs, sp, xdev, xr.at[a, 3 + d])
                push(a, o, fs, sp, cdev, cr.at[a, k, 3 + d])
    order = [(zf(d), d - 1) for d in (1, 3, 2)] + [(yf(d), 3 + d) for d in (0, 1, 3, 2)]
    def stage_x(a):
        for fs, i in order:
            sp = span(0, 1 - x, c)
            arrived(a, fs, sp, xr.at[a, i])
            push(a, outs[a].at[fs, sp], fs, sp, cdev, cr.at[a, 2, i])
    for a in range(n):
        stage_z(a)
        stage_y(a)
        stage_x(a)
    for a in range(n):
        for fs, i in order:
            for k, sp in ((0, span(0, x, 1 - c)), (1, span(1, x, 1 - c)), (2, span(0, 1 - x, 1 - c))):
                if k == 1 and not rest: continue
                arrived(a, fs, sp, cr.at[a, k, i])
        local[a].wait()
    for cp in sends:
        cp.wait_send()

def gather(*ws):
    n = len(ws)
    part = ws[0].shape[0] * 3 // 16
    D = pltpu.SemaphoreType.DMA
    return pl.pallas_call(functools.partial(gather_kernel, n, part),
        out_shape=[jax.ShapeDtypeStruct((8,) + w.shape, w.dtype) for w in ws],
        in_specs=[pl.BlockSpec(memory_space=pl.ANY)] * n,
        out_specs=[pl.BlockSpec(memory_space=pl.ANY)] * n,
        scratch_shapes=[D((n,)), D((n, 42)), D((n, 2, 3)), D((n, 2, 4)), D((n, 7)), D((n, 3, 7))],
        compiler_params=pltpu.CompilerParams(collective_id=0, has_side_effects=True),
        name="gather")(*ws)


def fits(count, width):
    return count == 8 and lax.axis_size("slide") == 4 and width % 256 == 0


def stacked(values, weight):
    out = jnp.einsum("tk,fkn->ftn", values, weight, preferred_element_type=jnp.float32)
    return out.astype(jnp.float32).transpose(1, 0, 2).reshape(values.shape[0], -1)


def on_device(tiles, tile_cell, tissue, norm_gain, qk_gain, row_qkv, row_out, col_qkv, col_out):
    count = lax.axis_size("fsdp")
    index = lax.axis_index("fsdp")
    width = tiles.shape[1]
    tok_dev = tiles.shape[0]
    slots = tok_dev // count
    if fits(count, width):
        row_qkv, row_out, col_qkv, col_out = gather(row_qkv, row_out, col_qkv, col_out)
    grid_rows = tissue.shape[0]
    columns = tissue.shape[1]
    rows_dev = grid_rows // count
    cols_dev = columns // count
    arrived = lax.all_to_all(
        tiles.reshape(count, slots, width), "fsdp", split_axis=0, concat_axis=0, tiled=True
    )
    table_cell = lax.dynamic_index_in_dim(
        tile_cell.reshape(count, count, slots), index, 1, keepdims=False
    )
    row_base = index * rows_dev
    local_cells = (table_cell - row_base * columns).reshape(-1)
    grid = (
        jnp.zeros((tok_dev, width), jnp.bfloat16)
        .at[local_cells]
        .set(arrived.reshape(tok_dev, width))
    )
    rows_pos = row_base + lax.broadcasted_iota(jnp.int32, (rows_dev, columns), 0)
    cols_pos = lax.broadcasted_iota(jnp.int32, (rows_dev, columns), 1)
    live_rows = lax.dynamic_slice_in_dim(tissue, row_base, rows_dev, 0)
    qkv = project_qkv(rms_norm(grid, norm_gain[0]), row_qkv).reshape(rows_dev, columns, 3 * width)
    mixed = attend(qkv, qk_gain[0], rows_pos, cols_pos, live_rows, False, HEADS)
    hidden = grid.astype(jnp.float32) + project_out(mixed.reshape(tok_dev, width), row_out)
    hidden = hidden.astype(jnp.bfloat16).reshape(rows_dev, columns, width)
    turned = lax.all_to_all(hidden, "fsdp", split_axis=1, concat_axis=0, tiled=True)
    col_base = index * cols_dev
    rows_pos_col = lax.broadcasted_iota(jnp.int32, (grid_rows, cols_dev), 0)
    cols_pos_col = col_base + lax.broadcasted_iota(jnp.int32, (grid_rows, cols_dev), 1)
    live_cols = lax.dynamic_slice_in_dim(tissue, col_base, cols_dev, 1)
    flat = turned.reshape(grid_rows * cols_dev, width)
    qkv_col = project_qkv(rms_norm(flat, norm_gain[1]), col_qkv).reshape(
        grid_rows, cols_dev, 3 * width
    )
    mixed_col = attend(qkv_col, qk_gain[1], rows_pos_col, cols_pos_col, live_cols, True, HEADS)
    result = flat.astype(jnp.float32) + project_out(
        mixed_col.reshape(grid_rows * cols_dev, width), col_out
    )
    return result.astype(jnp.bfloat16).reshape(grid_rows, cols_dev, width)


def solution(mesh):
    return jax.shard_map(
        on_device,
        mesh=mesh,
        in_specs=(
            P(("slide", "fsdp"), None),
            P("slide"),
            P("slide", None),
            P(),
            P(),
            P(None, "fsdp"),
            P(None, "fsdp"),
            P(None, "fsdp"),
            P(None, "fsdp"),
        ),
        out_specs=P("slide", "fsdp", None),
        check_vma=False,
    )
```

```python
import functools

import jax
import jax.numpy as jnp
from jax import lax
from jax.experimental import pallas as pl
from jax.experimental.pallas import tpu as pltpu
from jax.sharding import PartitionSpec as P

HEADS = 24
MESH = pl.DeviceIdType.MESH


EPS = 1e-06


def rms_norm(grid, gain):
    values = grid.astype(jnp.float32)
    scale = lax.rsqrt(jnp.mean(values * values, axis=-1, keepdims=True) + EPS)
    return (values * scale * gain).astype(jnp.bfloat16)


def head_norm(values, gain):
    scale = lax.rsqrt(jnp.mean(values * values, axis=-1, keepdims=True) + EPS)
    return values * scale * gain


def rotate(values, rows_pos, cols_pos):
    quarter = values.shape[-1] // 4
    freq = 10000.0 ** (-jnp.arange(quarter).astype(jnp.float32) / quarter)

    def turn(part, position):
        angle = position.astype(jnp.float32)[..., None, None] * freq
        cosine = jnp.cos(angle)
        sine = jnp.sin(angle)
        first = part[..., :quarter]
        second = part[..., quarter:]
        return jnp.concatenate(
            [first * cosine - second * sine, first * sine + second * cosine], axis=-1
        )

    half = 2 * quarter
    return jnp.concatenate(
        [turn(values[..., :half], rows_pos), turn(values[..., half:], cols_pos)], axis=-1
    )


def attend(qkv, gains, rows_pos, cols_pos, keys_live, column, heads):
    width = qkv.shape[-1] // 3
    size = width // heads
    if fits(lax.axis_size("fsdp"), width) and size == 64:
        return attend_pairs(qkv, gains, rows_pos, cols_pos, keys_live, column)
    shape = qkv.shape[:-1] + (heads, size)
    query = qkv[..., :width].reshape(shape).astype(jnp.float32)
    key = qkv[..., width : 2 * width].reshape(shape).astype(jnp.float32)
    value = qkv[..., 2 * width :].reshape(shape)
    query = rotate(head_norm(query, gains[0]), rows_pos, cols_pos).astype(jnp.bfloat16)
    key = rotate(head_norm(key, gains[1]), rows_pos, cols_pos).astype(jnp.bfloat16)
    if column:
        score_form = "lbhd,mbhd->bhlm"
        mix_form = "bhlm,mbhd->lbhd"
        live = keys_live.T
    else:
        score_form = "blhd,bmhd->bhlm"
        mix_form = "bhlm,bmhd->blhd"
        live = keys_live
    scores = jnp.einsum(score_form, query, key, preferred_element_type=jnp.float32) * size ** (-0.5)
    length = scores.shape[-1]
    diagonal = jnp.arange(length)[:, None] == jnp.arange(length)[None, :]
    allow = (live[:, None, None, :] > 0) | diagonal[None, None]
    scores = jnp.where(allow, scores, -1e30)
    top = jnp.max(scores, axis=-1, keepdims=True)
    weights = jnp.exp(scores - top)
    total = jnp.sum(weights, axis=-1)
    mixed = jnp.einsum(
        mix_form, weights.astype(jnp.bfloat16), value, preferred_element_type=jnp.float32
    )
    if column:
        total = total.transpose(2, 0, 1)
    else:
        total = total.transpose(0, 2, 1)
    return (mixed / total[..., None]).reshape(qkv.shape[:-1] + (width,)).astype(jnp.bfloat16)


def project_qkv(normed, weight):
    if weight.ndim == 3:
        return stacked(normed, weight).astype(jnp.bfloat16)

    def multiply(piece, start):
        return jnp.dot(normed, piece, preferred_element_type=jnp.float32)

    return multiply(lax.all_gather(weight, "fsdp", axis=1, tiled=True), jnp.int32(0)).astype(
        jnp.bfloat16
    )


def project_out(mixed, weight):
    if weight.ndim == 3:
        return stacked(mixed, weight)

    def multiply(piece, start):
        return jnp.dot(mixed, piece, preferred_element_type=jnp.float32)

    return multiply(lax.all_gather(weight, "fsdp", axis=1, tiled=True), jnp.int32(0))


def gather_kernel(n, part, *refs):
    ws, outs = refs[:n], refs[n:2*n]
    loc, send, zr, yr, xr, cr = refs[2*n:]
    s, f = lax.axis_index("slide"), lax.axis_index("fsdp")
    x, c, z, y = s // 2, s % 2, f // 2, f % 2
    zdev = lambda d: (lax.rem(z + d, 4) * 2 + y, s)
    ydev = (z * 2 + 1 - y, s)
    xdev = (f, (1 - x) * 2 + c)
    cdev = (f, x * 2 + 1 - c)
    bar = pltpu.get_barrier_semaphore()
    peers = [zdev(1), zdev(2), zdev(3), ydev, xdev, cdev]
    for p in peers:
        pl.semaphore_signal(bar, inc=1, device_id=p, device_id_type=MESH)
    pl.semaphore_wait(bar, len(peers))
    sends = []
    rows = ws[0].shape[0]
    rest = (rows - 4 * part) // 2
    def span(k, ax, ac):
        if k == 0:
            return pl.ds(pl.multiple_of((ax * 2 + ac) * part, 16), part)
        return pl.ds(pl.multiple_of(4 * part + ac * rest, 16), rest)
    kinds = (0, 1) if rest else (0,)
    count = [0] * n
    def push(a, src, fsrc, sp, dev, rsem):
        cp = pltpu.make_async_remote_copy(src_ref=src, dst_ref=outs[a].at[fsrc, sp], send_sem=send.at[a, count[a]],
            recv_sem=rsem, device_id=dev, device_id_type=MESH)
        count[a] += 1
        cp.start()
        sends.append(cp)
    def arrived(a, fsrc, sp, rsem):
        r = outs[a].at[fsrc, sp]
        pltpu.make_async_remote_copy(src_ref=r, dst_ref=r, send_sem=send.at[a, 0], recv_sem=rsem, device_id=cdev, device_id_type=MESH).wait_recv()
    local = []
    for a in range(n):
        for k in kinds:
            sp = span(k, x, c)
            for d in (1, 3, 2):
                push(a, ws[a].at[sp], f, sp, zdev(d), zr.at[a, k, d - 1])
            push(a, ws[a].at[sp], f, sp, ydev, yr.at[a, k, 0])
        cp = pltpu.make_async_copy(ws[a], outs[a].at[f], loc.at[a])
        cp.start()
        local.append(cp)
    zf = lambda d: lax.rem(z - d + 4, 4) * 2 + y
    yf = lambda d: lax.rem(z - d + 4, 4) * 2 + 1 - y
    def stage_z(a):
        for d in (1, 3, 2):
            fs = zf(d)
            for k in kinds:
                sp = span(k, x, c)
                arrived(a, fs, sp, zr.at[a, k, d - 1])
                o = outs[a].at[fs, sp]
                push(a, o, fs, sp, ydev, yr.at[a, k, d])
                if k == 0:
                    push(a, o, fs, sp, xdev, xr.at[a, d - 1])
                push(a, o, fs, sp, cdev, cr.at[a, k, d - 1])
    def stage_y(a):
        for d in (0, 1, 3, 2):
            fs = yf(d)
            for k in kinds:
                sp = span(k, x, c)
                arrived(a, fs, sp, yr.at[a, k, d])
                o = outs[a].at[fs, sp]
                if k == 0:
                    push(a, o, fs, sp, xdev, xr.at[a, 3 + d])
                push(a, o, fs, sp, cdev, cr.at[a, k, 3 + d])
    order = [(zf(d), d - 1) for d in (1, 3, 2)] + [(yf(d), 3 + d) for d in (0, 1, 3, 2)]
    def stage_x(a):
        for fs, i in order:
            sp = span(0, 1 - x, c)
            arrived(a, fs, sp, xr.at[a, i])
            push(a, outs[a].at[fs, sp], fs, sp, cdev, cr.at[a, 2, i])
    for a in range(n):
        stage_z(a)
        stage_y(a)
        stage_x(a)
    for a in range(n):
        for fs, i in order:
            for k, sp in ((0, span(0, x, 1 - c)), (1, span(1, x, 1 - c)), (2, span(0, 1 - x, 1 - c))):
                if k == 1 and not rest: continue
                arrived(a, fs, sp, cr.at[a, k, i])
        local[a].wait()
    for cp in sends:
        cp.wait_send()

def gather(*ws):
    n = len(ws)
    part = ws[0].shape[0] * 3 // 16
    D = pltpu.SemaphoreType.DMA
    return pl.pallas_call(functools.partial(gather_kernel, n, part),
        out_shape=[jax.ShapeDtypeStruct((8,) + w.shape, w.dtype) for w in ws],
        in_specs=[pl.BlockSpec(memory_space=pl.ANY)] * n,
        out_specs=[pl.BlockSpec(memory_space=pl.ANY)] * n,
        scratch_shapes=[D((n,)), D((n, 42)), D((n, 2, 3)), D((n, 2, 4)), D((n, 7)), D((n, 3, 7))],
        compiler_params=pltpu.CompilerParams(collective_id=0, has_side_effects=True),
        name="gather")(*ws)


def fits(count, width):
    return count == 8 and lax.axis_size("slide") == 4 and width % 256 == 0


def stacked(values, weight):
    out = jnp.einsum("tk,fkn->ftn", values, weight, preferred_element_type=jnp.float32)
    return out.astype(jnp.float32).transpose(1, 0, 2).reshape(values.shape[0], -1)


def attend_kernel(q_ref, k_ref, v_ref, bias_ref, cos_ref, sin_ref, gain_ref, o_ref):
    shape = q_ref.shape
    tokens = shape[0] * shape[1]
    lane = lax.broadcasted_iota(jnp.int32, (tokens, 128), 1)
    low = lane < 64
    front = (lane % 32) < 16
    cosine = cos_ref[...].reshape(tokens, 128)
    sine = sin_ref[...].reshape(tokens, 128)
    bias = bias_ref[0]

    def prepare(ref, which):
        t = ref[...].astype(jnp.float32).reshape(tokens, 128)
        square = t * t
        first = jnp.sum(jnp.where(low, square, 0.0), axis=1, keepdims=True)
        second = jnp.sum(jnp.where(low, 0.0, square), axis=1, keepdims=True)
        scale = lax.rsqrt(jnp.where(low, first, second) * (1.0 / 64.0) + EPS)
        t = t * scale * gain_ref[pl.ds(which, 1), :]
        partner = jnp.where(front, pltpu.roll(t, 112, 1), pltpu.roll(t, 16, 1))
        return (t * cosine + partner * sine).astype(jnp.bfloat16)

    query = prepare(q_ref, 0)
    key = prepare(k_ref, 1)
    value = v_ref[...].astype(jnp.float32).reshape(tokens, 128).astype(jnp.bfloat16)
    mixed = []
    for head in range(2):
        own = low if head == 0 else ~low
        one = jnp.where(own, query.astype(jnp.float32), 0.0).astype(jnp.bfloat16)
        scores = lax.dot_general(
            one, key, (((1,), (1,)), ((), ())), preferred_element_type=jnp.float32
        )
        scores = scores * 0.125 + bias
        weights = jnp.exp(scores - jnp.max(scores, axis=1, keepdims=True))
        total = jnp.sum(weights, axis=1, keepdims=True)
        part = jnp.dot(weights.astype(jnp.bfloat16), value, preferred_element_type=jnp.float32)
        mixed.append(part / total)
    o_ref[...] = jnp.where(low, mixed[0], mixed[1]).reshape(shape).astype(jnp.bfloat16)


def attend_pairs(qkv, gains, rows_pos, cols_pos, live, column):
    lead, second, wide = qkv.shape
    width = wide // 3
    pairs = width // 128
    quarter = 16
    freq = 10000.0 ** (-jnp.arange(quarter).astype(jnp.float32) / quarter)
    angles = [p.astype(jnp.float32)[..., None] * freq for p in (rows_pos, cols_pos)]
    cosine = jnp.concatenate([jnp.cos(a) for a in angles for _ in range(2)], axis=-1)
    sine = jnp.concatenate([v for a in angles for v in (-jnp.sin(a), jnp.sin(a))], axis=-1)
    cosine = jnp.concatenate([cosine, cosine], axis=-1)
    sine = jnp.concatenate([sine, sine], axis=-1)
    gain = jnp.concatenate([gains, gains], axis=-1)
    if column:
        block = (lead, 16, 128)
        groups, stride = second // 16, 16
        alive = live.reshape(lead, groups, 16).transpose(1, 0, 2).reshape(groups, lead * 16)
        place = lambda g, p: (0, g, p)
    else:
        block = (1, second, 128)
        groups, stride = lead, 1
        alive = live
        place = lambda g, p: (g, 0, p)
    tokens = block[0] * block[1]
    at = jnp.arange(tokens)
    same = (at[:, None] % stride) == (at[None, :] % stride)
    allow = same[None] & ((alive[:, None, :] > 0) | (at[:, None] == at[None, :])[None])
    bias = jnp.where(allow, 0.0, -1e30).astype(jnp.float32)
    spec = lambda off: pl.BlockSpec(block, lambda g, p: place(g, p + off))
    table = pl.BlockSpec(block, lambda g, p: place(g, 0))
    return pl.pallas_call(
        attend_kernel,
        grid=(groups, pairs),
        out_shape=jax.ShapeDtypeStruct((lead, second, width), jnp.bfloat16),
        in_specs=[
            spec(0),
            spec(pairs),
            spec(2 * pairs),
            pl.BlockSpec((1, tokens, tokens), lambda g, p: (g, 0, 0)),
            table,
            table,
            pl.BlockSpec((2, 128), lambda g, p: (0, 0)),
        ],
        out_specs=spec(0),
        compiler_params=pltpu.CompilerParams(vmem_limit_bytes=32 * 1024 * 1024),
        name="attend_column" if column else "attend_row",
    )(qkv, qkv, qkv, bias, cosine, sine, gain)


def on_device(tiles, tile_cell, tissue, norm_gain, qk_gain, row_qkv, row_out, col_qkv, col_out):
    count = lax.axis_size("fsdp")
    index = lax.axis_index("fsdp")
    width = tiles.shape[1]
    tok_dev = tiles.shape[0]
    slots = tok_dev // count
    if fits(count, width):
        row_qkv, row_out, col_qkv, col_out = gather(row_qkv, row_out, col_qkv, col_out)
    grid_rows = tissue.shape[0]
    columns = tissue.shape[1]
    rows_dev = grid_rows // count
    cols_dev = columns // count
    arrived = lax.all_to_all(
        tiles.reshape(count, slots, width), "fsdp", split_axis=0, concat_axis=0, tiled=True
    )
    table_cell = lax.dynamic_index_in_dim(
        tile_cell.reshape(count, count, slots), index, 1, keepdims=False
    )
    row_base = index * rows_dev
    local_cells = (table_cell - row_base * columns).reshape(-1)
    grid = (
        jnp.zeros((tok_dev, width), jnp.bfloat16)
        .at[local_cells]
        .set(arrived.reshape(tok_dev, width))
    )
    rows_pos = row_base + lax.broadcasted_iota(jnp.int32, (rows_dev, columns), 0)
    cols_pos = lax.broadcasted_iota(jnp.int32, (rows_dev, columns), 1)
    live_rows = lax.dynamic_slice_in_dim(tissue, row_base, rows_dev, 0)
    qkv = project_qkv(rms_norm(grid, norm_gain[0]), row_qkv).reshape(rows_dev, columns, 3 * width)
    mixed = attend(qkv, qk_gain[0], rows_pos, cols_pos, live_rows, False, HEADS)
    hidden = grid.astype(jnp.float32) + project_out(mixed.reshape(tok_dev, width), row_out)
    hidden = hidden.astype(jnp.bfloat16).reshape(rows_dev, columns, width)
    turned = lax.all_to_all(hidden, "fsdp", split_axis=1, concat_axis=0, tiled=True)
    col_base = index * cols_dev
    rows_pos_col = lax.broadcasted_iota(jnp.int32, (grid_rows, cols_dev), 0)
    cols_pos_col = col_base + lax.broadcasted_iota(jnp.int32, (grid_rows, cols_dev), 1)
    live_cols = lax.dynamic_slice_in_dim(tissue, col_base, cols_dev, 1)
    flat = turned.reshape(grid_rows * cols_dev, width)
    qkv_col = project_qkv(rms_norm(flat, norm_gain[1]), col_qkv).reshape(
        grid_rows, cols_dev, 3 * width
    )
    mixed_col = attend(qkv_col, qk_gain[1], rows_pos_col, cols_pos_col, live_cols, True, HEADS)
    result = flat.astype(jnp.float32) + project_out(
        mixed_col.reshape(grid_rows * cols_dev, width), col_out
    )
    return result.astype(jnp.bfloat16).reshape(grid_rows, cols_dev, width)


def solution(mesh):
    return jax.shard_map(
        on_device,
        mesh=mesh,
        in_specs=(
            P(("slide", "fsdp"), None),
            P("slide"),
            P("slide", None),
            P(),
            P(),
            P(None, "fsdp"),
            P(None, "fsdp"),
            P(None, "fsdp"),
            P(None, "fsdp"),
        ),
        out_specs=P("slide", "fsdp", None),
        check_vma=False,
    )
```
